32 devices in a mesh: groups: 2 (over x), expert: 16 (over z, y, core).
Axes of the slice: x: 2, y: 2, z: 4, core: 2. Of those that a mesh axis runs over, the one named last changes fastest.
Arguments:
- block_input: bfloat16 [2048, 1152], P(('groups', 'expert')), parts along dimension 0, may hold values from -6 to 6
- probe_bits: int32 [2048, 1152], P(('groups', 'expert')), parts along dimension 0, may hold values from 0 to 1
- query_rows: bfloat16 [2048, 1152], P(('groups', 'expert')), parts along dimension 0, may hold values from -8 to 8
- key_rows: bfloat16 [2048, 1152], P(('groups', 'expert')), parts along dimension 0, may hold values from -8 to 8
- value_rows: bfloat16 [2048, 1152], P(('groups', 'expert')), parts along dimension 0, may hold values from -6 to 6
- query_tangent: bfloat16 [2048, 1152], P(('groups', 'expert')), parts along dimension 0, may hold values from -6 to 6
- key_tangent: bfloat16 [2048, 1152], P(('groups', 'expert')), parts along dimension 0, may hold values from -6 to 6
- value_tangent: bfloat16 [2048, 1152], P(('groups', 'expert')), parts along dimension 0, may hold values from -6 to 6
- output_weight: bfloat16 [1152, 1152], replicated, may hold values from -0.1875 to 0.1875
- expert_up: bfloat16 [1152, 73728], P(None, 'expert'), may hold values from -0.1875 to 0.1875
- expert_down: bfloat16 [1152, 73728], P(None, 'expert'), may hold values from -0.09375 to 0.09375
- expert_ids: int32 [2048, 2], P(('groups', 'expert')), parts along dimension 0, may hold values from 0 to 15, all different within a row
- gate_weights: float32 [2048, 2], P(('groups', 'expert')), parts along dimension 0, may hold values from 0.1 to 0.9
Outputs:
- block_output: bfloat16 [2048, 1152], P(('groups', 'expert')), parts along dimension 0
- output_tangent: bfloat16 [2048, 1152], P(('groups', 'expert')), parts along dimension 0
- probe_dot: float32 [2048], P(('groups', 'expert')), parts along dimension 0
The draws below stay inside these ranges and needn't reach their ends.
There are 2 independent parts, one for each index of `groups`. The reference program is written for one: setup_inputs(seed, part) draws one part's arguments, and reference() takes and returns one part's arrays. A program takes and returns all parts, laid end to end along the dimension named above; an argument that names none is the same for every part. Nothing has to cross between parts.
Inputs may be any that keep to these rules, and one draw needn't show every extreme that they name: `expert_ids`: each row names 2 different experts.
All inputs are finite; a program needn't handle non-finite values.
Results may differ from the reference program's by a relative error of at most 0.0053.
Values may be sent and summed in bfloat16 or wider, within the bound.
A program may use at most 128 MiB of HBM per device.

```python
import jax
import jax.numpy as jnp
from jax import lax

D = 1152
HEADS = 16
EXPERTS = 16
TOP = 2
HID = 4608
LENGTH = 512
TOK_DEV = 64
TOKENS = 1024
REPL = 1
CAPACITY = 8


def draw_query_rows(key, part):
    key = jax.random.fold_in(key, 3)
    base = jnp.clip(jax.random.normal(key, (TOKENS, D), jnp.float32), -6.0, 6.0)
    return base.astype(jnp.bfloat16)


def draw_key_rows(key, part):
    key = jax.random.fold_in(key, 7)
    base = jnp.clip(jax.random.normal(key, (TOKENS, D), jnp.float32), -6.0, 6.0)
    return base.astype(jnp.bfloat16)


def set_ends(values, rng, low, top_value):
    extent = values.shape
    place = [jax.random.randint(jax.random.fold_in(rng, axis), (), 0, extent[axis]) for axis in range(len(extent))]
    values = values.at[tuple(place)].set(low)
    longest = extent.index(max(extent))
    place[longest] = (place[longest] + 1) % extent[longest]
    return values.at[tuple(place)].set(top_value)


def block_scale(rng, dims, cuts, low, largest):
    factor_of, own = 1.0, jax.random.fold_in(rng, 6)
    for dim, blocks in cuts:
        heights = jnp.exp(jax.random.uniform(jax.random.fold_in(own, dim), (blocks,), jnp.float32, low / len(cuts), largest / len(cuts)))
        factor_of = factor_of * jnp.repeat(heights, dims[dim] // blocks).reshape([-1 if axis == dim else 1 for axis in range(len(dims))])
    return factor_of


def distinct(own_key, rows, count, top, lift):
    ranking = jax.random.permutation(jax.random.fold_in(own_key, 1), count)
    pull = ranking
    for power in range(3):
        pull = pull * pull // count
    pull = pull * lift // count
    chance = jax.random.randint(jax.random.fold_in(own_key, 2), (rows, count), 0, 4096) + pull
    sure = jax.random.permutation(jax.random.fold_in(own_key, 3), rows)[jnp.arange(count) % rows]
    chance = jnp.where(jnp.arange(rows)[:, None] == sure[None, :], 1 << 14, chance)
    merit = chance * count + jnp.arange(count)
    return lax.top_k(merit.astype(jnp.int32), top)[1].astype(jnp.int32)


def bell_draw(own_key, dims, deviation, most, shards=(), kind=jnp.bfloat16):
    factor_of = block_scale(own_key, dims, shards, -0.22, 0.18) if shards else 1.0
    array = jax.random.normal(own_key, dims, jnp.float32) * deviation * factor_of
    return jnp.minimum(jnp.maximum(array, -most), most).astype(kind)


def setup_inputs(seed: int = 0, part: int = 0) -> dict:
    key_of = jax.random.split(jax.random.key(seed), 14)
    part_keys = jax.random.split(jax.random.fold_in(key_of[13], part), 14)
    block_input = bell_draw(part_keys[0], (TOKENS, D), 1.0, 6.0, ((0, 16),))
    probe_bits = set_ends(jax.random.randint(part_keys[1], (TOKENS, D), 0, 2), jax.random.fold_in(part_keys[1], 1), 0, 1).astype(jnp.int32)
    query_rows = draw_query_rows(jax.random.fold_in(jax.random.fold_in(key_of[13], part), 71), part)
    key_rows = draw_key_rows(jax.random.fold_in(jax.random.fold_in(key_of[13], part), 71), part)
    value_rows = bell_draw(part_keys[4], (TOKENS, D), 1.0, 6.0, ((0, 16),))
    query_tangent = bell_draw(part_keys[5], (TOKENS, D), 1.0, 6.0, ((0, 16),))
    key_tangent = bell_draw(part_keys[6], (TOKENS, D), 1.0, 6.0, ((0, 16),))
    value_tangent = bell_draw(part_keys[7], (TOKENS, D), 1.0, 6.0, ((0, 16),))
    output_weight = bell_draw(key_of[8], (D, D), D ** -0.5, 0.1875)
    expert_up = bell_draw(key_of[9], (D, EXPERTS * HID), D ** -0.5, 0.1875, ((1, 16),))
    expert_down = bell_draw(key_of[10], (D, EXPERTS * HID), HID ** -0.5, 0.09375, ((1, 16),))
    expert_ids = distinct(part_keys[11], TOKENS, EXPERTS, TOP, 1024)
    gate_weights = jnp.clip(0.1 + 0.79999997 * jax.random.uniform(part_keys[12], (TOKENS, TOP), jnp.float32) ** block_scale(part_keys[12], (TOKENS, TOP), ((0, 16),), -0.2, 0.2), 0.1, 0.9)
    return dict(block_input=block_input, probe_bits=probe_bits, query_rows=query_rows, key_rows=key_rows, value_rows=value_rows, query_tangent=query_tangent, key_tangent=key_tangent, value_tangent=value_tangent, output_weight=output_weight, expert_up=expert_up, expert_down=expert_down, expert_ids=expert_ids, gate_weights=gate_weights)


CUBIC_COEF = 0.044715
TANH_SCALE = 0.7978845608028654
NORM_EPS = 1e-06

def gelu_pair(preact):
    inner_arg = TANH_SCALE * (preact + CUBIC_COEF * preact * preact * preact)
    tanh_value = jnp.tanh(inner_arg)
    activation = 0.5 * preact * (1.0 + tanh_value)
    derivative = 0.5 * (1.0 + tanh_value) + 0.5 * preact * (1.0 - tanh_value * tanh_value) * TANH_SCALE * (1.0 + 3.0 * CUBIC_COEF * preact * preact)
    return (activation, derivative)

def norm_pair(hidden, tangent):
    average = lax.optimization_barrier(jnp.mean(hidden, axis=-1, keepdims=True))
    centered = hidden - average
    variance = lax.optimization_barrier(jnp.mean(centered * centered, axis=-1, keepdims=True))
    inverse = lax.rsqrt(variance + NORM_EPS)
    normed = centered * inverse
    tangent_centered = tangent - lax.optimization_barrier(jnp.mean(tangent, axis=-1, keepdims=True))
    normed_tangent = inverse * (tangent_centered - normed * lax.optimization_barrier(jnp.mean(normed * tangent_centered, axis=-1, keepdims=True)))
    return (normed, normed_tangent)

def rounded(source):
    return lax.optimization_barrier(source.astype(jnp.bfloat16)).astype(jnp.float32)

def attend_image(query_heads, key_heads, value_heads, query_slope, key_slope, value_slope):
    score_scale = (D // HEADS) ** (-0.5)
    scores = jnp.einsum('thd,shd->hts', query_heads, key_heads) * score_scale
    score_tangent = (jnp.einsum('thd,shd->hts', query_slope, key_heads) + jnp.einsum('thd,shd->hts', query_heads, key_slope)) * score_scale
    row_max = lax.optimization_barrier(jnp.max(scores, axis=-1, keepdims=True))
    exponent = jnp.exp(scores - row_max)
    weights = exponent / lax.optimization_barrier(jnp.sum(exponent, axis=-1, keepdims=True))
    weight_tangent = weights * (score_tangent - lax.optimization_barrier(jnp.sum(weights * score_tangent, axis=-1, keepdims=True)))
    weights_low = rounded(weights)
    tangent_low = rounded(weight_tangent)
    mixture = jnp.einsum('hts,shd->thd', weights_low, value_heads)
    mixture_tangent = jnp.einsum('hts,shd->thd', tangent_low, value_heads) + jnp.einsum('hts,shd->thd', weights_low, value_slope)
    return (mixture, mixture_tangent)

def block_sums(act_low, down_block):
    row_total = act_low.shape[0]
    part_units = HID // REPL
    pieces = jnp.einsum('rjh,djh->jrd', act_low.astype(jnp.float32).reshape(row_total, REPL, part_units), down_block.astype(jnp.float32).reshape(D, REPL, part_units))
    return lax.optimization_barrier(jnp.sum(rounded(pieces), axis=0))

def reference(block_input, probe_bits, query_rows, key_rows, value_rows, query_tangent, key_tangent, value_tangent, output_weight, expert_up, expert_down, expert_ids, gate_weights):
    images = TOKENS // LENGTH
    head_dim = D // HEADS

    def per_image(image_index):

        def select_image(source):
            start = (image_index * LENGTH).astype(jnp.int32)
            return lax.dynamic_slice_in_dim(source, start, LENGTH, 0).astype(jnp.float32).reshape(LENGTH, HEADS, head_dim)
        return attend_image(select_image(query_rows), select_image(key_rows), select_image(value_rows), select_image(query_tangent), select_image(key_tangent), select_image(value_tangent))
    mixture, mixture_tangent = lax.map(per_image, jnp.arange(images, dtype=jnp.int32))
    mixture = mixture.reshape(TOKENS, D).astype(jnp.bfloat16)
    mixture_tangent = mixture_tangent.reshape(TOKENS, D).astype(jnp.bfloat16)
    sign_values = (2 * probe_bits - 1).astype(jnp.float32)
    hidden = block_input.astype(jnp.float32) + jnp.dot(mixture, output_weight, preferred_element_type=jnp.float32)
    hidden_tangent = sign_values + jnp.dot(mixture_tangent, output_weight, preferred_element_type=jnp.float32)
    normed, normed_tangent = norm_pair(hidden, hidden_tangent)
    normed_low = normed.astype(jnp.bfloat16)
    normed_slope = normed_tangent.astype(jnp.bfloat16)
    blocks = TOKENS // TOK_DEV
    pairs = TOK_DEV * TOP
    flat_ids = expert_ids.reshape(blocks, pairs)
    one_hot = (flat_ids[:, :, None] == jnp.arange(EXPERTS, dtype=jnp.int32)[None, None, :]).astype(jnp.int32)
    running = jnp.cumsum(one_hot, axis=1).astype(jnp.int32) - 1
    order_rank = lax.optimization_barrier(jnp.sum(one_hot * running, axis=2)).astype(jnp.int32)
    retained = order_rank < CAPACITY
    block_index = jnp.arange(blocks, dtype=jnp.int32)[:, None]
    slot_index = (block_index * CAPACITY + order_rank).astype(jnp.int32)
    token_index = (block_index * TOK_DEV + jnp.arange(pairs, dtype=jnp.int32)[None, :] // TOP).astype(jnp.int32)
    slot_table = jnp.full((EXPERTS, blocks * CAPACITY), TOKENS, jnp.int32)
    target_slot = jnp.where(retained, slot_index, blocks * CAPACITY).astype(jnp.int32)
    slot_table = slot_table.at[flat_ids.reshape(-1), target_slot.reshape(-1)].set(token_index.reshape(-1), mode='drop')
    padded_rows = jnp.concatenate([normed_low, jnp.zeros((1, D), jnp.bfloat16)], axis=0)
    padded_slope = jnp.concatenate([normed_slope, jnp.zeros((1, D), jnp.bfloat16)], axis=0)

    def expert_pass(expert_index):
        chosen = slot_table[expert_index]
        expert_rows = padded_rows[chosen]
        tangent_rows = padded_slope[chosen]
        start = (expert_index * HID).astype(jnp.int32)
        up_block = lax.dynamic_slice_in_dim(expert_up, start, HID, 1)
        down_block = lax.dynamic_slice_in_dim(expert_down, start, HID, 1)
        preact = jnp.dot(expert_rows, up_block, preferred_element_type=jnp.float32)
        preact_tangent = jnp.dot(tangent_rows, up_block, preferred_element_type=jnp.float32)
        activation, derivative = gelu_pair(preact)
        act_low = activation.astype(jnp.bfloat16)
        act_slope = (derivative * preact_tangent).astype(jnp.bfloat16)
        return (block_sums(act_low, down_block), block_sums(act_slope, down_block))
    produced, produced_tangent = lax.map(expert_pass, jnp.arange(EXPERTS, dtype=jnp.int32))
    safe_slot = jnp.where(retained, slot_index, 0).astype(jnp.int32)
    gate_kept = jnp.where(retained, gate_weights.reshape(blocks, pairs), jnp.float32(0.0))
    picked = produced[flat_ids, safe_slot] * gate_kept[:, :, None]
    picked_tangent = produced_tangent[flat_ids, safe_slot] * gate_kept[:, :, None]
    expert_mix = lax.optimization_barrier(jnp.sum(picked.reshape(TOKENS, TOP, D), axis=1))
    expert_mix_tangent = lax.optimization_barrier(jnp.sum(picked_tangent.reshape(TOKENS, TOP, D), axis=1))
    block_output = (hidden + expert_mix).astype(jnp.bfloat16)
    full_tangent = hidden_tangent + expert_mix_tangent
    probe_dot = lax.optimization_barrier(jnp.sum(sign_values * full_tangent, axis=1)) * D ** (-0.5)
    return (block_output, full_tangent.astype(jnp.bfloat16), probe_dot)
```

```python
import functools

import jax
import jax.numpy as jnp
from jax import lax
from jax.experimental import pallas as pl
from jax.experimental.pallas import tpu as pltpu
from jax.sharding import PartitionSpec as P

D = 1152
HEADS = 16
EXPERTS = 16
TOP = 2
LENGTH = 512
HEAD_DIM = D // HEADS
PAIR = 16

CUBIC_COEF = 0.044715
TANH_SCALE = 0.7978845608028654
NORM_EPS = 1e-06
LOG2E = 1.4426950408889634
F32 = jnp.float32
BF16 = jnp.bfloat16
MESH = pl.DeviceIdType.MESH


def gelu_pair(preact):
    square = preact * preact
    tanh_value = jnp.tanh(TANH_SCALE * preact * (1.0 + CUBIC_COEF * square))
    half = 0.5 * (1.0 + tanh_value)
    activation = preact * half
    derivative = half + (0.5 * TANH_SCALE) * preact * (1.0 - tanh_value * tanh_value) * (
        1.0 + 3.0 * CUBIC_COEF * square
    )
    return (activation, derivative)


def norm_pair(hidden, tangent):
    average = jnp.mean(hidden, axis=-1, keepdims=True)
    centered = hidden - average
    variance = jnp.mean(centered * centered, axis=-1, keepdims=True)
    inverse = lax.rsqrt(variance + NORM_EPS)
    normed = centered * inverse
    tangent_centered = tangent - jnp.mean(tangent, axis=-1, keepdims=True)
    normed_tangent = inverse * (
        tangent_centered - normed * jnp.mean(normed * tangent_centered, axis=-1, keepdims=True)
    )
    return (normed, normed_tangent)


def slot_choice(ids, gates, lanes, shift):
    tok = ids.shape[0]
    lane = lax.broadcasted_iota(jnp.int32, (tok, lanes), 1)
    named = lane >> shift
    first = ids[:, 0:1] == named
    second = ids[:, 1:2] == named
    has = jnp.where(first, 1.0, jnp.where(second, 1.0, 0.0))
    gate = jnp.where(first, gates[:, 0:1], jnp.where(second, gates[:, 1:2], 0.0))
    row = lax.broadcasted_iota(jnp.int32, (tok, tok), 0)
    column = lax.broadcasted_iota(jnp.int32, (tok, tok), 1)
    earlier = jnp.where(column < row, 1.0, 0.0).astype(BF16)
    rank = jnp.dot(earlier, has.astype(BF16), preferred_element_type=F32)
    picked = jnp.where(rank == (lane & 7).astype(F32), has, 0.0)
    tangent_lane = (lane & 8) != 0
    main = jnp.where(tangent_lane, 0.0, picked)
    slope = jnp.where(tangent_lane, picked, 0.0)
    return main, slope, gate


def kernel(
    n,
    block_ref, bits_ref, q_ref, k_ref, v_ref, dq_ref, dk_ref, dv_ref, ids_ref, gates_ref,
    wo_hbm, up_hbm, down_hbm,
    out_ref, tan_ref, dot_ref,
    wo, up, down,
    pack_send, pack_recv, mix_send, mix_recv, hidden, slots, rows_in, act, made, rows_back,
    load_sem, pack_ss, pack_rs, mix_ss, mix_rs, disp_ss, near_rs, far_rs, back_ss, back_rs,
):
    tok = block_ref.shape[0]
    near = LENGTH // tok
    owners = n // EXPERTS
    hid = up.shape[1]
    cols = D // near
    me = lax.axis_index("expert")
    pos = lax.rem(me, near)
    base = me - pos

    def send(src, dst, send_sem, recv_sem, device):
        pltpu.make_async_remote_copy(
            src_ref=src, dst_ref=dst, send_sem=send_sem, recv_sem=recv_sem,
            device_id={"expert": device}, device_id_type=MESH,
        ).start()

    def wait_bytes(ref, sem):
        pltpu.make_async_copy(ref, ref, sem).wait()

    barrier = pltpu.get_barrier_semaphore()

    @pl.loop(1, n)
    def _(k):
        pl.semaphore_signal(
            barrier, inc=1, device_id={"expert": lax.rem(me + k, n)}, device_id_type=MESH
        )

    loads = [
        pltpu.make_async_copy(wo_hbm, wo, load_sem.at[0]),
        pltpu.make_async_copy(up_hbm, up, load_sem.at[1]),
        pltpu.make_async_copy(down_hbm, down, load_sem.at[2]),
    ]
    for load in loads:
        load.start()

    parts = [ref[...] for ref in (k_ref, dk_ref, dq_ref, q_ref, v_ref, dv_ref)]
    pad = jnp.zeros((tok, pack_send.shape[2] - 6 * cols), BF16)
    for j in range(near):
        pieces = []
        for pair in (parts[0:2], parts[2:4], parts[4:6]):
            for start in range(j * cols, (j + 1) * cols, HEAD_DIM):
                pieces += [part[:, start : start + HEAD_DIM] for part in pair]
        pack_send[j] = jnp.concatenate(pieces + [pad], axis=1)

    pl.semaphore_wait(barrier, n - 1)

    @pl.loop(1, near)
    def _(k):
        j = lax.rem(pos + k, near)
        send(
            pack_send.at[j], pack_recv.at[pl.ds(pl.multiple_of(pos * tok, tok), tok)],
            pack_ss, pack_rs, base + j,
        )

    pack_recv[pl.ds(pl.multiple_of(pos * tok, tok), tok), :] = pack_send[pos]
    wait_bytes(pack_recv.at[pl.ds(0, (near - 1) * tok)], pack_rs)

    local_heads = HEADS // near
    double = 2 * HEAD_DIM
    tail = 4 * cols // 128 * 128
    values_t = pack_recv[:, tail:].T
    tile = 2 * tok

    @pl.loop(0, near // 2)
    def _(i):
        rows = pl.ds(pl.multiple_of(i * tile, tile), tile)
        mains, slopes = [], []
        for h in range(local_heads):
            keys = pack_recv[:, h * double : (h + 1) * double]
            queries = pack_recv[rows, 2 * cols + h * double : 2 * cols + (h + 1) * double]
            alone = jnp.concatenate(
                [queries[:, HEAD_DIM:], jnp.zeros((tile, HEAD_DIM), BF16)], axis=1
            )
            both = lax.dot_general(
                keys, jnp.concatenate([alone, queries], axis=0),
                (((1,), (1,)), ((), ())), preferred_element_type=F32,
            )
            scores, slope = both[:, :tile], both[:, tile:]
            top = jnp.max(scores, axis=0, keepdims=True)
            exponent = jnp.exp2((scores - top) * (HEAD_DIM ** (-0.5) * LOG2E))
            inverse = 1.0 / jnp.sum(exponent, axis=0, keepdims=True)
            weights = exponent * inverse
            middle = jnp.sum(weights * slope, axis=0, keepdims=True)
            weight_slope = weights * ((slope - middle) * HEAD_DIM ** (-0.5))
            joined = jnp.concatenate([weights.astype(BF16), weight_slope.astype(BF16)], axis=1)
            start = 4 * cols - tail + h * double
            mixed = jnp.dot(
                values_t[start : start + double], joined, preferred_element_type=F32
            )
            mains.append(mixed[:HEAD_DIM, :tile])
            slopes.append(mixed[HEAD_DIM:, :tile] + mixed[:HEAD_DIM, tile:])
        main = jnp.concatenate(mains, axis=0)
        slope = jnp.concatenate(slopes, axis=0)
        for half in range(2):
            j = i * 2 + half
            lanes = slice(half * tok, (half + 1) * tok)
            mix_send[j] = jnp.concatenate([main[:, lanes], slope[:, lanes]], axis=1).astype(BF16)

            @pl.when(j != pos)
            def _():
                send(
                    mix_send.at[j], mix_recv.at[pl.ds(pl.multiple_of(pos * cols, 16), cols)],
                    mix_ss, mix_rs, base + j,
                )

    mix_recv[pl.ds(pl.multiple_of(pos * cols, 16), cols), :] = mix_send[pos]
    main_pick, slope_pick, _ = slot_choice(ids_ref[...], gates_ref[...], EXPERTS * PAIR, 4)
    pick = jnp.concatenate([main_pick, slope_pick], axis=0).astype(BF16)
    signs = (2 * bits_ref[...] - 1).astype(F32)
    loads[0].wait()
    wait_bytes(mix_recv.at[pl.ds(0, (near - 1) * cols)], mix_rs)

    hidden[...] = lax.dot_general(
        mix_recv[...], wo[...], (((0,), (0,)), ((), ())), preferred_element_type=F32
    )
    hidden[:tok] += block_ref[...].astype(F32)
    hidden[tok:] += signs
    normed, normed_slope = norm_pair(hidden[:tok], hidden[tok:])
    slots[...] = lax.dot_general(
        pick, jnp.concatenate([normed.astype(BF16), normed_slope.astype(BF16)], axis=0),
        (((0,), (0,)), ((), ())), preferred_element_type=F32,
    ).astype(BF16)

    mine = pl.ds(pl.multiple_of(me * PAIR, PAIR), PAIR)

    def slot_rows(device):
        return pl.ds(pl.multiple_of(device // owners * PAIR, PAIR), PAIR)

    @pl.loop(0, n - near)
    def _(k):
        group = lax.rem(base + near * (1 + k // near), n)
        device = group + lax.rem(pos + k, near)
        send(slots.at[slot_rows(device)], rows_in.at[mine], disp_ss, far_rs, device)

    @pl.loop(1, near)
    def _(k):
        device = base + lax.rem(pos + k, near)
        send(slots.at[slot_rows(device)], rows_in.at[mine], disp_ss, near_rs, device)

    rows_in[mine, :] = slots[slot_rows(me), :]

    up_step = 768 if hid % 768 == 0 else hid
    down_step = 384
    block_rows = near * PAIR

    def expert_block(group):
        start = pl.multiple_of(group * PAIR, block_rows)

        @pl.loop(0, hid // up_step)
        def _(c):
            span = pl.ds(pl.multiple_of(c * up_step, 128), up_step) if hid > up_step else pl.ds(0, hid)
            preact = jnp.dot(
                rows_in[pl.ds(start, block_rows), :], up[:, span], preferred_element_type=F32
            ).reshape(near, PAIR, up_step)
            activation, derivative = gelu_pair(preact[:, :8])
            both = jnp.concatenate([activation, derivative * preact[:, 8:]], axis=1)
            act[:, span] = both.reshape(block_rows, up_step).astype(BF16)

        @pl.loop(0, D // down_step)
        def _(c):
            span = pl.ds(pl.multiple_of(c * down_step, 128), down_step)
            made[pl.ds(start, block_rows), span] = lax.dot_general(
                act[...], down[span, :], (((1,), (1,)), ((), ())), preferred_element_type=F32
            ).astype(BF16)

            @pl.loop(0, near)
            def _(k):
                device = group + lax.rem(pos + k, near)
                source = made.at[pl.ds(pl.multiple_of(device * PAIR, PAIR), PAIR), span]

                @pl.when(device != me)
                def _():
                    send(source, rows_back.at[mine, span], back_ss, back_rs, device)

    loads[1].wait()
    loads[2].wait()
    wait_bytes(rows_in.at[pl.ds(0, (near - 1) * PAIR)], near_rs)
    expert_block(base)
    rows_back[mine, :] = made[mine, :]
    wait_bytes(rows_in.at[pl.ds(0, (n - near) * PAIR)], far_rs)

    @pl.loop(1, n // near)
    def _(g):
        expert_block(lax.rem(base + g * near, n))

    shift = 3 + (PAIR * owners // 8).bit_length() - 1
    main_pick, slope_pick, gate = slot_choice(ids_ref[...], gates_ref[...], n * PAIR, shift)
    mixing = jnp.concatenate([main_pick * gate, slope_pick * gate], axis=0)
    high = mixing.astype(BF16)
    low = (mixing - high.astype(F32)).astype(BF16)
    signs = (2 * bits_ref[...] - 1).astype(F32)
    wait_bytes(rows_back.at[pl.ds(0, (n - 1) * PAIR)], back_rs)

    full = (
        hidden[...]
        + jnp.dot(high, rows_back[...], preferred_element_type=F32)
        + jnp.dot(low, rows_back[...], preferred_element_type=F32)
    )
    out_ref[...] = full[:tok].astype(BF16)
    full_slope = full[tok:]
    tan_ref[...] = full_slope.astype(BF16)
    column = jnp.sum(signs * full_slope, axis=1, keepdims=True) * D ** (-0.5)
    eye = lax.broadcasted_iota(jnp.int32, (tok, tok), 0) == lax.broadcasted_iota(
        jnp.int32, (tok, tok), 1
    )
    dot_ref[...] = jnp.sum(jnp.where(eye, column, 0.0), axis=0, keepdims=True)

    wait_bytes(pack_send.at[pl.ds(0, near - 1)], pack_ss)
    wait_bytes(mix_send.at[pl.ds(0, near - 1)], mix_ss)
    wait_bytes(rows_in.at[pl.ds(0, (n - 1) * PAIR)], disp_ss)
    wait_bytes(made.at[pl.ds(0, (n - 1) * PAIR)], back_ss)


def per_device(
    n,
    block_input,
    probe_bits,
    query_rows,
    key_rows,
    value_rows,
    query_tangent,
    key_tangent,
    value_tangent,
    output_weight,
    expert_up,
    expert_down,
    expert_ids,
    gate_weights,
):
    tok = block_input.shape[0]
    assert tok * TOP // EXPERTS == 8
    hid = expert_up.shape[1]
    near = LENGTH // tok
    cols = D // near
    packed = -(-6 * cols // 128) * 128
    vmem = pl.BlockSpec(memory_space=pltpu.VMEM)
    anywhere = pl.BlockSpec(memory_space=pl.ANY)
    dma = pltpu.SemaphoreType.DMA
    macs = 2 * n * PAIR * D * hid + tok * D * (6 * LENGTH + 2 * D)
    block_output, output_tangent, probe_dot = pl.pallas_call(
        functools.partial(kernel, n),
        out_shape=(
            jax.ShapeDtypeStruct((tok, D), BF16),
            jax.ShapeDtypeStruct((tok, D), BF16),
            jax.ShapeDtypeStruct((1, tok), F32),
        ),
        in_specs=[vmem] * 10 + [anywhere] * 3,
        out_specs=(vmem, vmem, vmem),
        scratch_shapes=[
            pltpu.VMEM((D, D), BF16),
            pltpu.VMEM((D, hid), BF16),
            pltpu.VMEM((D, hid), BF16),
            pltpu.VMEM((near, tok, packed), BF16),
            pltpu.VMEM((LENGTH, packed), BF16),
            pltpu.VMEM((near, cols, 2 * tok), BF16),
            pltpu.VMEM((D, 2 * tok), BF16),
            pltpu.VMEM((2 * tok, D), F32),
            pltpu.VMEM((EXPERTS * PAIR, D), BF16),
            pltpu.VMEM((n * PAIR, D), BF16),
            pltpu.VMEM((near * PAIR, hid), BF16),
            pltpu.VMEM((n * PAIR, D), BF16),
            pltpu.VMEM((n * PAIR, D), BF16),
            dma((3,)),
        ]
        + [dma] * 9,
        compiler_params=pltpu.CompilerParams(
            collective_id=0, has_side_effects=True, vmem_limit_bytes=56 * 1024 * 1024
        ),
        cost_estimate=pl.CostEstimate(
            flops=2 * macs, bytes_accessed=4 * D * hid + 2 * D * D, transcendentals=tok * D * 64
        ),
    )(
        block_input, probe_bits, query_rows, key_rows, value_rows,
        query_tangent, key_tangent, value_tangent, expert_ids, gate_weights,
        output_weight, expert_up, expert_down,
    )
    return (block_output, output_tangent, probe_dot.reshape(tok))


def solution(mesh):
    token_rows = P(("groups", "expert"), None)
    return jax.shard_map(
        functools.partial(per_device, mesh.shape["expert"]),
        mesh=mesh,
        in_specs=(token_rows,) * 8
        + (P(), P(None, "expert"), P(None, "expert"), token_rows, token_rows),
        out_specs=(token_rows, token_rows, P(("groups", "expert"))),
        check_vma=False,
    )
```

```python
import functools

import jax
import jax.numpy as jnp
from jax import lax
from jax.experimental import pallas as pl
from jax.experimental.pallas import tpu as pltpu
from jax.sharding import PartitionSpec as P

D = 1152
HEADS = 16
EXPERTS = 16
TOP = 2
LENGTH = 512
HEAD_DIM = D // HEADS
PAIR = 16

CUBIC_COEF = 0.044715
TANH_SCALE = 0.7978845608028654
NORM_EPS = 1e-06
LOG2E = 1.4426950408889634
F32 = jnp.float32
BF16 = jnp.bfloat16
MESH = pl.DeviceIdType.MESH


def gelu_pair(preact):
    square = preact * preact
    tanh_value = jnp.tanh(TANH_SCALE * preact * (1.0 + CUBIC_COEF * square))
    half = 0.5 * (1.0 + tanh_value)
    activation = preact * half
    derivative = half + (0.5 * TANH_SCALE) * preact * (1.0 - tanh_value * tanh_value) * (
        1.0 + 3.0 * CUBIC_COEF * square
    )
    return (activation, derivative)


def norm_pair(hidden, tangent):
    average = jnp.mean(hidden, axis=-1, keepdims=True)
    centered = hidden - average
    variance = jnp.mean(centered * centered, axis=-1, keepdims=True)
    inverse = lax.rsqrt(variance + NORM_EPS)
    normed = centered * inverse
    tangent_centered = tangent - jnp.mean(tangent, axis=-1, keepdims=True)
    normed_tangent = inverse * (
        tangent_centered - normed * jnp.mean(normed * tangent_centered, axis=-1, keepdims=True)
    )
    return (normed, normed_tangent)


def slot_choice(ids, gates, slots, shift):
    tok = ids.shape[1]
    slot = lax.broadcasted_iota(jnp.int32, (slots, tok), 0)
    named = slot >> shift
    first = ids[0:1, :] == named
    second = ids[1:2, :] == named
    has = jnp.where(first, 1.0, jnp.where(second, 1.0, 0.0))
    gate = jnp.where(first, gates[0:1, :], jnp.where(second, gates[1:2, :], 0.0))
    row = lax.broadcasted_iota(jnp.int32, (tok, tok), 0)
    column = lax.broadcasted_iota(jnp.int32, (tok, tok), 1)
    earlier = jnp.where(row < column, 1.0, 0.0).astype(BF16)
    rank = jnp.dot(has.astype(BF16), earlier, preferred_element_type=F32)
    picked = jnp.where(rank == (slot & 7).astype(F32), has, 0.0)
    tangent_slot = (slot & 8) != 0
    main = jnp.where(tangent_slot, 0.0, picked)
    slope = jnp.where(tangent_slot, picked, 0.0)
    return jnp.concatenate([main, slope], axis=1), jnp.concatenate([gate, gate], axis=1)


def kernel(
    n,
    k_hbm, dk_hbm, dq_hbm, q_hbm, v_hbm, dv_hbm, block_hbm, bits_hbm, ids_hbm, gates_hbm,
    wo_hbm, up_hbm, down_hbm,
    out_hbm, tan_hbm, dot_hbm,
    k_ref, dk_ref, dq_ref, q_ref, v_ref, dv_ref, block_ref, bits_ref, ids_ref, gates_ref,
    wo, up, down, out_ref, tan_ref, dot_ref,
    pack_send, pack_recv, probs, mix_send, mix_recv, hidden, pick, mix_high, mix_low,
    slots, rows_in, act, made, rows_back,
    load_sem, out_sem,
    pack_ss, score_rs, value_rs, mix_ss, mix_rs, disp_ss, early_rs, late_rs, back_ss, back_rs,
):
    tok = block_ref.shape[0]
    near = LENGTH // tok
    far = n - near
    owners = n // EXPERTS
    hid = up.shape[1]
    cols = D // near
    me = lax.axis_index("expert")
    pos = lax.rem(me, near)
    base = me - pos

    def send(src, dst, send_sem, recv_sem, device):
        pltpu.make_async_remote_copy(
            src_ref=src, dst_ref=dst, send_sem=send_sem, recv_sem=recv_sem,
            device_id={"expert": device}, device_id_type=MESH,
        ).start()

    def wait_bytes(ref, sem):
        pltpu.make_async_copy(ref, ref, sem).wait()

    barrier = pltpu.get_barrier_semaphore()

    @pl.loop(1, n)
    def _(k):
        pl.semaphore_signal(
            barrier, inc=1, device_id={"expert": lax.rem(me + k, n)}, device_id_type=MESH
        )

    pairs = [
        (k_hbm, k_ref), (dk_hbm, dk_ref), (dq_hbm, dq_ref), (q_hbm, q_ref), (v_hbm, v_ref),
        (dv_hbm, dv_ref), (ids_hbm, ids_ref), (gates_hbm, gates_ref), (block_hbm, block_ref),
        (bits_hbm, bits_ref), (wo_hbm, wo), (up_hbm, up), (down_hbm, down),
    ]
    loads = [
        pltpu.make_async_copy(src, dst, load_sem.at[i]) for i, (src, dst) in enumerate(pairs)
    ]
    for load in loads:
        load.start()
    for load in loads[:6]:
        load.wait()

    parts = [ref[...] for ref in (k_ref, dk_ref, dq_ref, q_ref, v_ref, dv_ref)]
    packed = pack_send.shape[2]
    pad = jnp.zeros((tok, packed - 6 * cols), BF16)
    for j in range(near):
        pieces = []
        for pair in (parts[0:2], parts[2:4], parts[4:6]):
            for start in range(j * cols, (j + 1) * cols, HEAD_DIM):
                pieces += [part[:, start : start + HEAD_DIM] for part in pair]
        pack_send[j] = jnp.concatenate(pieces + [pad], axis=1)

    pl.semaphore_wait(barrier, n - 1)

    score_cols = -(-4 * cols // 128) * 128
    score_part = pl.ds(0, score_cols)
    value_part = pl.ds(score_cols, packed - score_cols)
    my_tokens = pl.ds(pl.multiple_of(pos * tok, tok), tok)
    for part, sem in ((score_part, score_rs), (value_part, value_rs)):

        @pl.loop(1, near)
        def _(k):
            j = lax.rem(pos + k, near)
            send(
                pack_send.at[j, :, part], pack_recv.at[my_tokens, part], pack_ss, sem, base + j
            )

    pack_recv[my_tokens, :] = pack_send[pos]

    loads[6].wait()
    loads[7].wait()
    picked, _ = slot_choice(ids_ref[...], gates_ref[...], EXPERTS * PAIR, 4)
    pick[...] = picked.astype(BF16)
    picked, gate = slot_choice(
        ids_ref[...], gates_ref[...], n * PAIR, 4 + owners.bit_length() - 1
    )
    mixing = (picked * gate).T
    high = mixing.astype(BF16)
    mix_high[...] = high
    mix_low[...] = (mixing - high.astype(F32)).astype(BF16)

    local_heads = HEADS // near
    double = 2 * HEAD_DIM
    tile = 2 * tok
    wait_bytes(pack_recv.at[pl.ds(0, (near - 1) * tok), score_part], score_rs)
    keys = [pack_recv[:, h * double : (h + 1) * double] for h in range(local_heads)]

    @pl.loop(0, near // 2, unroll=2)
    def _(i):
        rows = pl.ds(pl.multiple_of(i * tile, tile), tile)
        for h in range(local_heads):
            queries = pack_recv[rows, 2 * cols + h * double : 2 * cols + (h + 1) * double]
            alone = jnp.concatenate(
                [queries[:, HEAD_DIM:], jnp.zeros((tile, HEAD_DIM), BF16)], axis=1
            )
            both = lax.dot_general(
                keys[h], jnp.concatenate([alone, queries], axis=0),
                (((1,), (1,)), ((), ())), preferred_element_type=F32,
            )
            scores, slope = both[:, :tile], both[:, tile:]
            top = jnp.max(scores, axis=0, keepdims=True)
            exponent = jnp.exp2((scores - top) * (HEAD_DIM ** (-0.5) * LOG2E))
            inverse = 1.0 / jnp.sum(exponent, axis=0, keepdims=True)
            middle = jnp.sum(exponent * slope, axis=0, keepdims=True) * inverse
            probs[i * local_heads + h, :, :tile] = (exponent * inverse).astype(BF16)
            probs[i * local_heads + h, :, tile:] = (
                exponent * (inverse * HEAD_DIM ** (-0.5)) * (slope - middle)
            ).astype(BF16)

    wait_bytes(pack_recv.at[pl.ds(0, (near - 1) * tok), value_part], value_rs)
    tail = 4 * cols // 128 * 128
    values_t = pack_recv[:, tail:].T

    @pl.loop(0, near // 2, unroll=2)
    def _(i):
        mains, slopes = [], []
        for h in range(local_heads):
            start = 4 * cols - tail + h * double
            mixed = jnp.dot(
                values_t[start : start + double], probs[i * local_heads + h],
                preferred_element_type=F32,
            )
            mains.append(mixed[:HEAD_DIM, :tile])
            slopes.append(mixed[HEAD_DIM:, :tile] + mixed[:HEAD_DIM, tile:])
        main = jnp.concatenate(mains, axis=0)
        slope = jnp.concatenate(slopes, axis=0)
        for half in range(2):
            j = i * 2 + half
            lanes = slice(half * tok, (half + 1) * tok)
            mix_send[j] = jnp.concatenate([main[:, lanes], slope[:, lanes]], axis=1).astype(BF16)

            @pl.when(j != pos)
            def _():
                send(
                    mix_send.at[j], mix_recv.at[pl.ds(pl.multiple_of(pos * cols, 16), cols)],
                    mix_ss, mix_rs, base + j,
                )

    mix_recv[pl.ds(pl.multiple_of(pos * cols, 16), cols), :] = mix_send[pos]
    for load in loads[8:11]:
        load.wait()
    wait_bytes(mix_recv.at[pl.ds(0, (near - 1) * cols)], mix_rs)

    hidden[...] = lax.dot_general(
        mix_recv[...], wo[...], (((0,), (0,)), ((), ())), preferred_element_type=F32
    )
    signs = (2 * bits_ref[...] - 1).astype(F32)
    hidden[:tok] += block_ref[...].astype(F32)
    hidden[tok:] += signs
    normed, normed_slope = norm_pair(hidden[:tok], hidden[tok:])
    slots[...] = jnp.dot(
        pick[...],
        jnp.concatenate([normed.astype(BF16), normed_slope.astype(BF16)], axis=0),
        preferred_element_type=F32,
    ).astype(BF16)

    mine = pl.ds(pl.multiple_of(me * PAIR, PAIR), PAIR)

    def slot_rows(device):
        return pl.ds(pl.multiple_of(device // owners * PAIR, PAIR), PAIR)

    def place(t):
        return pl.ds(pl.multiple_of(t * PAIR, PAIR), PAIR)

    def partner(t, sign):
        group = lax.rem(base + n + sign * near * (1 + t // near), n)
        return group + lax.rem(pos + near + sign * lax.rem(t, near), near)

    def dispatch(t, sem):
        device = partner(t, 1)
        send(slots.at[slot_rows(device)], rows_in.at[place(t)], disp_ss, sem, device)

    @pl.loop(0, far // 2)
    def _(t):
        dispatch(t, early_rs)

    @pl.loop(far + 1, n)
    def _(t):
        dispatch(t, late_rs)

    @pl.loop(far // 2, far)
    def _(t):
        dispatch(t, late_rs)

    rows_in[place(far), :] = slots[slot_rows(me), :]

    up_step = 768 if hid % 768 == 0 else hid
    down_step = 384

    def expert_pass(first, last):
        count = (last - first) * PAIR
        block = count if count <= 256 else 4 * PAIR

        @pl.loop(0, count // block)
        def _(b):
            here = pl.ds(pl.multiple_of(b * block, 16), block)
            source = pl.ds(pl.multiple_of(first * PAIR + b * block, 16), block)

            @pl.loop(0, hid // up_step, unroll=min(2, hid // up_step))
            def _(c):
                span = (
                    pl.ds(pl.multiple_of(c * up_step, 128), up_step)
                    if hid > up_step
                    else pl.ds(0, hid)
                )
                preact = jnp.dot(
                    rows_in[source, :], up[:, span], preferred_element_type=F32
                ).reshape(block // PAIR, PAIR, up_step)
                activation, derivative = gelu_pair(preact[:, :8])
                both = jnp.concatenate([activation, derivative * preact[:, 8:]], axis=1)
                act[here, span] = both.reshape(block, up_step).astype(BF16)

        @pl.loop(0, D // down_step)
        def _(c):
            span = pl.ds(pl.multiple_of(c * down_step, 128), down_step)

            @pl.loop(0, count // block)
            def _(b):
                here = pl.ds(pl.multiple_of(b * block, 16), block)
                target = pl.ds(pl.multiple_of(first * PAIR + b * block, 16), block)
                made[target, span] = lax.dot_general(
                    act[here, :], down[span, :], (((1,), (1,)), ((), ())),
                    preferred_element_type=F32,
                ).astype(BF16)

            @pl.loop(first, last)
            def _(t):
                @pl.when(t != far)
                def _():
                    send(
                        made.at[place(t), span], rows_back.at[mine, span],
                        back_ss, back_rs, partner(t, -1),
                    )

    wait_bytes(rows_in.at[pl.ds(0, far // 2 * PAIR)], early_rs)
    loads[11].wait()
    loads[12].wait()
    expert_pass(0, far // 2)
    wait_bytes(rows_in.at[pl.ds(0, (n - 1 - far // 2) * PAIR)], late_rs)
    expert_pass(far // 2, n)
    rows_back[mine, :] = made[place(far), :]
    signs = (2 * bits_ref[...] - 1).astype(F32)
    wait_bytes(rows_back.at[pl.ds(0, (n - 1) * PAIR)], back_rs)

    full = (
        hidden[...]
        + jnp.dot(mix_high[...], rows_back[...], preferred_element_type=F32)
        + jnp.dot(mix_low[...], rows_back[...], preferred_element_type=F32)
    )
    out_ref[...] = full[:tok].astype(BF16)
    full_slope = full[tok:]
    tan_ref[...] = full_slope.astype(BF16)
    column = jnp.sum(signs * full_slope, axis=1, keepdims=True) * D ** (-0.5)
    eye = lax.broadcasted_iota(jnp.int32, (tok, tok), 0) == lax.broadcasted_iota(
        jnp.int32, (tok, tok), 1
    )
    dot_ref[...] = jnp.sum(jnp.where(eye, column, 0.0), axis=0, keepdims=True)
    stores = [
        pltpu.make_async_copy(src, dst, out_sem.at[i])
        for i, (src, dst) in enumerate(
            [(out_ref, out_hbm), (tan_ref, tan_hbm), (dot_ref, dot_hbm)]
        )
    ]
    for store in stores:
        store.start()
    wait_bytes(pack_send.at[pl.ds(0, near - 1)], pack_ss)
    wait_bytes(mix_send.at[pl.ds(0, near - 1)], mix_ss)
    wait_bytes(rows_in.at[pl.ds(0, (n - 1) * PAIR)], disp_ss)
    wait_bytes(made.at[pl.ds(0, (n - 1) * PAIR)], back_ss)
    for store in stores:
        store.wait()


def place_results(a_ref, b_ref, c_ref, x_ref, y_ref, z_ref, sem):
    moves = [
        pltpu.make_async_copy(src, dst, sem.at[i])
        for i, (src, dst) in enumerate([(a_ref, x_ref), (b_ref, y_ref), (c_ref, z_ref)])
    ]
    for move in moves:
        move.start()
    for move in moves:
        move.wait()


def per_device(
    n,
    block_input,
    probe_bits,
    query_rows,
    key_rows,
    value_rows,
    query_tangent,
    key_tangent,
    value_tangent,
    output_weight,
    expert_up,
    expert_down,
    expert_ids,
    gate_weights,
):
    tok = block_input.shape[0]
    assert tok * TOP // EXPERTS == 8
    hid = expert_up.shape[1]
    near = LENGTH // tok
    far = n - near
    cols = D // near
    packed = -(-6 * cols // 128) * 128
    anywhere = pl.BlockSpec(memory_space=pl.ANY)
    dma = pltpu.SemaphoreType.DMA
    macs = 2 * n * PAIR * D * hid + tok * D * (6 * LENGTH + 2 * D)
    results = (
        jax.ShapeDtypeStruct((tok, D), BF16),
        jax.ShapeDtypeStruct((tok, D), BF16),
        jax.ShapeDtypeStruct((1, tok), F32),
    )
    made = pl.pallas_call(
        functools.partial(kernel, n),
        out_shape=results,
        in_specs=[anywhere] * 13,
        out_specs=(anywhere,) * 3,
        scratch_shapes=[pltpu.VMEM((tok, D), BF16)] * 7
        + [
            pltpu.VMEM((tok, D), jnp.int32),
            pltpu.VMEM((TOP, tok), jnp.int32),
            pltpu.VMEM((TOP, tok), F32),
            pltpu.VMEM((D, D), BF16),
            pltpu.VMEM((D, hid), BF16),
            pltpu.VMEM((D, hid), BF16),
            pltpu.VMEM((tok, D), BF16),
            pltpu.VMEM((tok, D), BF16),
            pltpu.VMEM((1, tok), F32),
            pltpu.VMEM((near, tok, packed), BF16),
            pltpu.VMEM((LENGTH, packed), BF16),
            pltpu.VMEM((HEADS // 2, LENGTH, 4 * tok), BF16),
            pltpu.VMEM((near, cols, 2 * tok), BF16),
            pltpu.VMEM((D, 2 * tok), BF16),
            pltpu.VMEM((2 * tok, D), F32),
            pltpu.VMEM((EXPERTS * PAIR, 2 * tok), BF16),
            pltpu.VMEM((2 * tok, n * PAIR), BF16),
            pltpu.VMEM((2 * tok, n * PAIR), BF16),
            pltpu.VMEM((EXPERTS * PAIR, D), BF16),
            pltpu.VMEM((n * PAIR, D), BF16),
            pltpu.VMEM(((n - far // 2) * PAIR, hid), BF16),
            pltpu.VMEM((n * PAIR, D), BF16),
            pltpu.VMEM((n * PAIR, D), BF16),
            dma((13,)),
            dma((3,)),
        ]
        + [dma] * 10,
        compiler_params=pltpu.CompilerParams(
            collective_id=0, has_side_effects=True, vmem_limit_bytes=56 * 1024 * 1024
        ),
        cost_estimate=pl.CostEstimate(
            flops=2 * macs, bytes_accessed=4 * D * hid + 2 * D * D, transcendentals=tok * D * 64
        ),
    )(
        key_rows, key_tangent, query_tangent, query_rows, value_rows, value_tangent,
        block_input, probe_bits, expert_ids.T, gate_weights.T,
        output_weight, expert_up, expert_down,
    )
    block_output, output_tangent, probe_dot = pl.pallas_call(
        place_results,
        out_shape=results,
        in_specs=[anywhere] * 3,
        out_specs=(anywhere,) * 3,
        scratch_shapes=[dma((3,))],
    )(*made)
    return (block_output, output_tangent, probe_dot.reshape(tok))


def solution(mesh):
    token_rows = P(("groups", "expert"), None)
    return jax.shard_map(
        functools.partial(per_device, mesh.shape["expert"]),
        mesh=mesh,
        in_specs=(token_rows,) * 8
        + (P(), P(None, "expert"), P(None, "expert"), token_rows, token_rows),
        out_specs=(token_rows, token_rows, P(("groups", "expert"))),
        check_vma=False,
    )
```

```python
import functools

import jax
import jax.numpy as jnp
from jax import lax
from jax.experimental import pallas as pl
from jax.experimental.pallas import tpu as pltpu
from jax.sharding import PartitionSpec as P

D = 1152
HEADS = 16
EXPERTS = 16
TOP = 2
LENGTH = 512
HEAD_DIM = D // HEADS
PAIR = 16

CUBIC_COEF = 0.044715
TANH_SCALE = 0.7978845608028654
NORM_EPS = 1e-06
LOG2E = 1.4426950408889634
F32 = jnp.float32
BF16 = jnp.bfloat16
MESH = pl.DeviceIdType.MESH


def gelu_pair(preact):
    square = preact * preact
    tanh_value = jnp.tanh(TANH_SCALE * preact * (1.0 + CUBIC_COEF * square))
    half = 0.5 * (1.0 + tanh_value)
    activation = preact * half
    derivative = half + (0.5 * TANH_SCALE) * preact * (1.0 - tanh_value * tanh_value) * (
        1.0 + 3.0 * CUBIC_COEF * square
    )
    return (activation, derivative)


def norm_pair(hidden, tangent):
    average = jnp.mean(hidden, axis=-1, keepdims=True)
    centered = hidden - average
    variance = jnp.mean(centered * centered, axis=-1, keepdims=True)
    inverse = lax.rsqrt(variance + NORM_EPS)
    normed = centered * inverse
    tangent_centered = tangent - jnp.mean(tangent, axis=-1, keepdims=True)
    normed_tangent = inverse * (
        tangent_centered - normed * jnp.mean(normed * tangent_centered, axis=-1, keepdims=True)
    )
    return (normed, normed_tangent)


def slot_choice(ids, gates, slots, shift):
    tok = ids.shape[1]
    slot = lax.broadcasted_iota(jnp.int32, (slots, tok), 0)
    named = slot >> shift
    first = ids[0:1, :] == named
    second = ids[1:2, :] == named
    has = jnp.where(first, 1.0, jnp.where(second, 1.0, 0.0))
    gate = jnp.where(first, gates[0:1, :], jnp.where(second, gates[1:2, :], 0.0))
    row = lax.broadcasted_iota(jnp.int32, (tok, tok), 0)
    column = lax.broadcasted_iota(jnp.int32, (tok, tok), 1)
    earlier = jnp.where(row < column, 1.0, 0.0).astype(BF16)
    rank = jnp.dot(has.astype(BF16), earlier, preferred_element_type=F32)
    picked = jnp.where(rank == (slot & 7).astype(F32), has, 0.0)
    tangent_slot = (slot & 8) != 0
    main = jnp.where(tangent_slot, 0.0, picked)
    slope = jnp.where(tangent_slot, picked, 0.0)
    return jnp.concatenate([main, slope], axis=1), jnp.concatenate([gate, gate], axis=1)


def kernel(
    n,
    k_hbm, dk_hbm, dq_hbm, q_hbm, v_hbm, dv_hbm, block_hbm, bits_hbm, ids_hbm, gates_hbm,
    wo_hbm, up_hbm, down_hbm,
    out_hbm, tan_hbm, dot_hbm,
    k_ref, dk_ref, dq_ref, q_ref, v_ref, dv_ref, block_ref, bits_ref, ids_ref, gates_ref,
    wo, up, down, out_ref, tan_ref, dot_ref,
    pack_send, pack_recv, probs, mix_send, mix_recv, hidden, pick, mix_high, mix_low,
    slots, rows_in, act, made, rows_back,
    load_sem, out_sem,
    pack_ss, score_rs, value_rs, mix_ss, mix_rs, disp_ss, early_rs, late_rs, back_ss, back_rs,
):
    tok = block_ref.shape[0]
    near = LENGTH // tok
    far = n - near
    owners = n // EXPERTS
    hid = up.shape[1]
    cols = D // near
    me = lax.axis_index("expert")
    pos = lax.rem(me, near)
    base = me - pos

    def send(src, dst, send_sem, recv_sem, device):
        pltpu.make_async_remote_copy(
            src_ref=src, dst_ref=dst, send_sem=send_sem, recv_sem=recv_sem,
            device_id={"expert": device}, device_id_type=MESH,
        ).start()

    def wait_bytes(ref, sem):
        pltpu.make_async_copy(ref, ref, sem).wait()

    barrier = pltpu.get_barrier_semaphore()

    @pl.loop(1, n)
    def _(k):
        pl.semaphore_signal(
            barrier, inc=1, device_id={"expert": lax.rem(me + k, n)}, device_id_type=MESH
        )

    pairs = [
        (k_hbm, k_ref), (dk_hbm, dk_ref), (dq_hbm, dq_ref), (q_hbm, q_ref), (v_hbm, v_ref),
        (dv_hbm, dv_ref), (ids_hbm, ids_ref), (gates_hbm, gates_ref), (block_hbm, block_ref),
        (bits_hbm, bits_ref), (wo_hbm, wo), (up_hbm, up), (down_hbm, down),
    ]
    loads = [
        pltpu.make_async_copy(src, dst, load_sem.at[i]) for i, (src, dst) in enumerate(pairs)
    ]
    for load in loads:
        load.start()
    for load in loads[:6]:
        load.wait()

    parts = [ref[...] for ref in (k_ref, dk_ref, dq_ref, q_ref, v_ref, dv_ref)]
    packed = pack_send.shape[2]
    pad = jnp.zeros((tok, packed - 6 * cols), BF16)
    for j in range(near):
        pieces = []
        for pair in (parts[0:2], parts[2:4], parts[4:6]):
            for start in range(j * cols, (j + 1) * cols, HEAD_DIM):
                pieces += [part[:, start : start + HEAD_DIM] for part in pair]
        pack_send[j] = jnp.concatenate(pieces + [pad], axis=1)

    pl.semaphore_wait(barrier, n - 1)

    score_cols = -(-4 * cols // 128) * 128
    score_part = pl.ds(0, score_cols)
    value_part = pl.ds(score_cols, packed - score_cols)
    my_tokens = pl.ds(pl.multiple_of(pos * tok, tok), tok)
    for part, sem in ((score_part, score_rs), (value_part, value_rs)):

        @pl.loop(1, near)
        def _(k):
            j = lax.rem(pos + k, near)
            send(
                pack_send.at[j, :, part], pack_recv.at[my_tokens, part], pack_ss, sem, base + j
            )

    pack_recv[my_tokens, :] = pack_send[pos]

    loads[6].wait()
    loads[7].wait()
    picked, _ = slot_choice(ids_ref[...], gates_ref[...], EXPERTS * PAIR, 4)
    pick[...] = picked.astype(BF16)
    picked, gate = slot_choice(
        ids_ref[...], gates_ref[...], n * PAIR, 4 + owners.bit_length() - 1
    )
    mixing = (picked * gate).T
    high = mixing.astype(BF16)
    mix_high[...] = high
    mix_low[...] = (mixing - high.astype(F32)).astype(BF16)

    local_heads = HEADS // near
    double = 2 * HEAD_DIM
    tile = 2 * tok
    wait_bytes(pack_recv.at[pl.ds(0, (near - 1) * tok), score_part], score_rs)
    keys = [pack_recv[:, h * double : (h + 1) * double] for h in range(local_heads)]

    @pl.loop(0, near // 2, unroll=2)
    def _(i):
        rows = pl.ds(pl.multiple_of(i * tile, tile), tile)
        for h in range(local_heads):
            queries = pack_recv[rows, 2 * cols + h * double : 2 * cols + (h + 1) * double]
            alone = jnp.concatenate(
                [queries[:, HEAD_DIM:], jnp.zeros((tile, HEAD_DIM), BF16)], axis=1
            )
            both = lax.dot_general(
                keys[h], jnp.concatenate([alone, queries], axis=0),
                (((1,), (1,)), ((), ())), preferred_element_type=F32,
            )
            scores, slope = both[:, :tile], both[:, tile:]
            top = jnp.max(scores, axis=0, keepdims=True)
            exponent = jnp.exp2((scores - top) * (HEAD_DIM ** (-0.5) * LOG2E))
            inverse = 1.0 / jnp.sum(exponent, axis=0, keepdims=True)
            middle = jnp.sum(exponent * slope, axis=0, keepdims=True) * inverse
            probs[i * local_heads + h, :, :tile] = (exponent * inverse).astype(BF16)
            probs[i * local_heads + h, :, tile:] = (
                exponent * (inverse * HEAD_DIM ** (-0.5)) * (slope - middle)
            ).astype(BF16)

    wait_bytes(pack_recv.at[pl.ds(0, (near - 1) * tok), value_part], value_rs)
    tail = 4 * cols // 128 * 128
    values_t = pack_recv[:, tail:].T

    @pl.loop(0, near // 2, unroll=2)
    def _(i):
        mains, slopes = [], []
        for h in range(local_heads):
            start = 4 * cols - tail + h * double
            mixed = jnp.dot(
                values_t[start : start + double], probs[i * local_heads + h],
                preferred_element_type=F32,
            )
            mains.append(mixed[:HEAD_DIM, :tile])
            slopes.append(mixed[HEAD_DIM:, :tile] + mixed[:HEAD_DIM, tile:])
        main = jnp.concatenate(mains, axis=0)
        slope = jnp.concatenate(slopes, axis=0)
        for half in range(2):
            j = i * 2 + half
            lanes = slice(half * tok, (half + 1) * tok)
            mix_send[j] = jnp.concatenate([main[:, lanes], slope[:, lanes]], axis=1).astype(BF16)

            @pl.when(j != pos)
            def _():
                send(
                    mix_send.at[j], mix_recv.at[pl.ds(pl.multiple_of(pos * cols, 16), cols)],
                    mix_ss, mix_rs, base + j,
                )

    mix_recv[pl.ds(pl.multiple_of(pos * cols, 16), cols), :] = mix_send[pos]
    for load in loads[8:11]:
        load.wait()
    wait_bytes(mix_recv.at[pl.ds(0, (near - 1) * cols)], mix_rs)

    hidden[...] = lax.dot_general(
        mix_recv[...], wo[...], (((0,), (0,)), ((), ())), preferred_element_type=F32
    )
    signs = (2 * bits_ref[...] - 1).astype(F32)
    hidden[:tok] += block_ref[...].astype(F32)
    hidden[tok:] += signs
    normed, normed_slope = norm_pair(hidden[:tok], hidden[tok:])
    slots[...] = jnp.dot(
        pick[...],
        jnp.concatenate([normed.astype(BF16), normed_slope.astype(BF16)], axis=0),
        preferred_element_type=F32,
    ).astype(BF16)

    mine = pl.ds(pl.multiple_of(me * PAIR, PAIR), PAIR)
    half = far // 2

    def slot_rows(device):
        return pl.ds(pl.multiple_of(device // owners * PAIR, PAIR), PAIR)

    def place(u):
        return pl.ds(pl.multiple_of(u * PAIR, PAIR), PAIR)

    def partner(t, sign):
        group = lax.rem(base + n + sign * near * (1 + t // near), n)
        return group + lax.rem(pos + near + sign * lax.rem(t, near), near)

    def dispatch(t, u, sem):
        device = partner(t, 1)
        send(slots.at[slot_rows(device)], rows_in.at[place(u)], disp_ss, sem, device)

    def give_back(t, u, span):
        send(
            made.at[place(u), span], rows_back.at[mine, span],
            back_ss, back_rs, partner(t, -1),
        )

    for k in range(near):
        if k < half:
            dispatch(k, k, early_rs)
        else:
            dispatch(k, k + near, late_rs)
        if k + 1 < near:
            dispatch(far + 1 + k, half + 1 + k, early_rs)

    @pl.loop(near, max(near, half))
    def _(t):
        dispatch(t, t, early_rs)

    @pl.loop(max(near, half), far)
    def _(t):
        dispatch(t, t + near, late_rs)

    rows_in[place(half), :] = slots[slot_rows(me), :]

    up_step = 768 if hid % 768 == 0 else hid
    every = pl.ds(0, D)

    def expert_pass(first, last, send_chunk):
        count = (last - first) * PAIR
        block = count if count <= 256 else 4 * PAIR

        @pl.loop(0, count // block)
        def _(b):
            here = pl.ds(pl.multiple_of(b * block, 16), block)
            source = pl.ds(pl.multiple_of(first * PAIR + b * block, 16), block)

            @pl.loop(0, hid // up_step, unroll=min(2, hid // up_step))
            def _(c):
                span = (
                    pl.ds(pl.multiple_of(c * up_step, 128), up_step)
                    if hid > up_step
                    else pl.ds(0, hid)
                )
                preact = jnp.dot(
                    rows_in[source, :], up[:, span], preferred_element_type=F32
                ).reshape(block // PAIR, PAIR, up_step)
                activation, derivative = gelu_pair(preact[:, :8])
                both = jnp.concatenate([activation, derivative * preact[:, 8:]], axis=1)
                act[here, span] = both.reshape(block, up_step).astype(BF16)

        for start, width in ((0, 512), (512, 512), (1024, 128)):
            span = pl.ds(start, width)

            @pl.loop(0, count // block)
            def _(b):
                here = pl.ds(pl.multiple_of(b * block, 16), block)
                target = pl.ds(pl.multiple_of(first * PAIR + b * block, 16), block)
                made[target, span] = lax.dot_general(
                    act[here, :], down[span, :], (((1,), (1,)), ((), ())),
                    preferred_element_type=F32,
                ).astype(BF16)

            send_chunk(span)

    def keep(span):
        pass

    def send_late(span):
        @pl.loop(half, far)
        def _(t):
            give_back(t, t + near, span)

    wait_bytes(rows_in.at[pl.ds(0, (half + near - 1) * PAIR)], early_rs)
    loads[11].wait()
    loads[12].wait()
    expert_pass(0, half + near, keep)
    wait_bytes(rows_in.at[pl.ds(0, (far - half) * PAIR)], late_rs)

    @pl.loop(0, half)
    def _(t):
        give_back(t, t, every)

    @pl.loop(1, near)
    def _(k):
        give_back(far + k, half + k, every)

    rows_back[mine, :] = made[place(half), :]
    expert_pass(half + near, n, send_late)
    signs = (2 * bits_ref[...] - 1).astype(F32)
    wait_bytes(rows_back.at[pl.ds(0, (n - 1) * PAIR)], back_rs)

    full = (
        hidden[...]
        + jnp.dot(mix_high[...], rows_back[...], preferred_element_type=F32)
        + jnp.dot(mix_low[...], rows_back[...], preferred_element_type=F32)
    )
    out_ref[...] = full[:tok].astype(BF16)
    full_slope = full[tok:]
    tan_ref[...] = full_slope.astype(BF16)
    column = jnp.sum(signs * full_slope, axis=1, keepdims=True) * D ** (-0.5)
    eye = lax.broadcasted_iota(jnp.int32, (tok, tok), 0) == lax.broadcasted_iota(
        jnp.int32, (tok, tok), 1
    )
    dot_ref[...] = jnp.sum(jnp.where(eye, column, 0.0), axis=0, keepdims=True)
    stores = [
        pltpu.make_async_copy(src, dst, out_sem.at[i])
        for i, (src, dst) in enumerate(
            [(out_ref, out_hbm), (tan_ref, tan_hbm), (dot_ref, dot_hbm)]
        )
    ]
    for store in stores:
        store.start()
    wait_bytes(pack_send.at[pl.ds(0, near - 1)], pack_ss)
    wait_bytes(mix_send.at[pl.ds(0, near - 1)], mix_ss)
    wait_bytes(rows_in.at[pl.ds(0, (n - 1) * PAIR)], disp_ss)
    wait_bytes(made.at[pl.ds(0, (n - 1) * PAIR)], back_ss)
    for store in stores:
        store.wait()


def place_results(a_hbm, b_hbm, c_hbm, x_hbm, y_hbm, z_hbm, a_ref, b_ref, c_ref, sem):
    moves = []
    for i, (src, held, dst) in enumerate(
        [(a_hbm, a_ref, x_hbm), (b_hbm, b_ref, y_hbm), (c_hbm, c_ref, z_hbm)]
    ):
        moves.append(
            (
                pltpu.make_async_copy(src, held, sem.at[i]),
                pltpu.make_async_copy(held, dst, sem.at[3 + i]),
            )
        )
    for load, _ in moves:
        load.start()
    for load, store in moves:
        load.wait()
        store.start()
    for _, store in moves:
        store.wait()


def per_device(
    n,
    block_input,
    probe_bits,
    query_rows,
    key_rows,
    value_rows,
    query_tangent,
    key_tangent,
    value_tangent,
    output_weight,
    expert_up,
    expert_down,
    expert_ids,
    gate_weights,
):
    tok = block_input.shape[0]
    assert tok * TOP // EXPERTS == 8
    hid = expert_up.shape[1]
    near = LENGTH // tok
    far = n - near
    cols = D // near
    packed = -(-6 * cols // 128) * 128
    anywhere = pl.BlockSpec(memory_space=pl.ANY)
    dma = pltpu.SemaphoreType.DMA
    macs = 2 * n * PAIR * D * hid + tok * D * (6 * LENGTH + 2 * D)
    results = (
        jax.ShapeDtypeStruct((tok, D), BF16),
        jax.ShapeDtypeStruct((tok, D), BF16),
        jax.ShapeDtypeStruct((1, tok), F32),
    )
    made = pl.pallas_call(
        functools.partial(kernel, n),
        out_shape=results,
        in_specs=[anywhere] * 13,
        out_specs=(anywhere,) * 3,
        scratch_shapes=[pltpu.VMEM((tok, D), BF16)] * 7
        + [
            pltpu.VMEM((tok, D), jnp.int32),
            pltpu.VMEM((TOP, tok), jnp.int32),
            pltpu.VMEM((TOP, tok), F32),
            pltpu.VMEM((D, D), BF16),
            pltpu.VMEM((D, hid), BF16),
            pltpu.VMEM((D, hid), BF16),
            pltpu.VMEM((tok, D), BF16),
            pltpu.VMEM((tok, D), BF16),
            pltpu.VMEM((1, tok), F32),
            pltpu.VMEM((near, tok, packed), BF16),
            pltpu.VMEM((LENGTH, packed), BF16),
            pltpu.VMEM((HEADS // 2, LENGTH, 4 * tok), BF16),
            pltpu.VMEM((near, cols, 2 * tok), BF16),
            pltpu.VMEM((D, 2 * tok), BF16),
            pltpu.VMEM((2 * tok, D), F32),
            pltpu.VMEM((EXPERTS * PAIR, 2 * tok), BF16),
            pltpu.VMEM((2 * tok, n * PAIR), BF16),
            pltpu.VMEM((2 * tok, n * PAIR), BF16),
            pltpu.VMEM((EXPERTS * PAIR, D), BF16),
            pltpu.VMEM((n * PAIR, D), BF16),
            pltpu.VMEM(((far // 2 + near) * PAIR, hid), BF16),
            pltpu.VMEM((n * PAIR, D), BF16),
            pltpu.VMEM((n * PAIR, D), BF16),
            dma((13,)),
            dma((3,)),
        ]
        + [dma] * 10,
        compiler_params=pltpu.CompilerParams(
            collective_id=0, has_side_effects=True, vmem_limit_bytes=56 * 1024 * 1024
        ),
        cost_estimate=pl.CostEstimate(
            flops=2 * macs, bytes_accessed=4 * D * hid + 2 * D * D, transcendentals=tok * D * 64
        ),
    )(
        key_rows, key_tangent, query_tangent, query_rows, value_rows, value_tangent,
        block_input, probe_bits, expert_ids.T, gate_weights.T,
        output_weight, expert_up, expert_down,
    )
    block_output, output_tangent, probe_dot = pl.pallas_call(
        place_results,
        out_shape=results,
        in_specs=[anywhere] * 3,
        out_specs=(anywhere,) * 3,
        scratch_shapes=[
            pltpu.VMEM((tok, D), BF16),
            pltpu.VMEM((tok, D), BF16),
            pltpu.VMEM((1, tok), F32),
            dma((6,)),
        ],
    )(*made)
    return (block_output, output_tangent, probe_dot.reshape(tok))


def solution(mesh):
    token_rows = P(("groups", "expert"), None)
    return jax.shard_map(
        functools.partial(per_device, mesh.shape["expert"]),
        mesh=mesh,
        in_specs=(token_rows,) * 8
        + (P(), P(None, "expert"), P(None, "expert"), token_rows, token_rows),
        out_specs=(token_rows, token_rows, P(("groups", "expert"))),
        check_vma=False,
    )
```

```python
import functools

import jax
import jax.numpy as jnp
from jax import lax
from jax.experimental import pallas as pl
from jax.experimental.pallas import tpu as pltpu
from jax.sharding import PartitionSpec as P

D = 1152
HEADS = 16
EXPERTS = 16
TOP = 2
LENGTH = 512
HEAD_DIM = D // HEADS
PAIR = 16

CUBIC_COEF = 0.044715
TANH_SCALE = 0.7978845608028654
NORM_EPS = 1e-06
LOG2E = 1.4426950408889634
F32 = jnp.float32
BF16 = jnp.bfloat16
MESH = pl.DeviceIdType.MESH


def gelu_pair(preact):
    square = preact * preact
    tanh_value = jnp.tanh(TANH_SCALE * preact * (1.0 + CUBIC_COEF * square))
    half = 0.5 * (1.0 + tanh_value)
    activation = preact * half
    derivative = half + (0.5 * TANH_SCALE) * preact * (1.0 - tanh_value * tanh_value) * (
        1.0 + 3.0 * CUBIC_COEF * square
    )
    return (activation, derivative)


def norm_pair(hidden, tangent):
    average = jnp.mean(hidden, axis=-1, keepdims=True)
    centered = hidden - average
    variance = jnp.mean(centered * centered, axis=-1, keepdims=True)
    inverse = lax.rsqrt(variance + NORM_EPS)
    normed = centered * inverse
    tangent_centered = tangent - jnp.mean(tangent, axis=-1, keepdims=True)
    normed_tangent = inverse * (
        tangent_centered - normed * jnp.mean(normed * tangent_centered, axis=-1, keepdims=True)
    )
    return (normed, normed_tangent)


def slot_choice(ids, gates, slots, shift):
    tok = ids.shape[1]
    slot = lax.broadcasted_iota(jnp.int32, (slots, tok), 0)
    named = slot >> shift
    first = ids[0:1, :] == named
    second = ids[1:2, :] == named
    has = jnp.where(first, 1.0, jnp.where(second, 1.0, 0.0))
    gate = jnp.where(first, gates[0:1, :], jnp.where(second, gates[1:2, :], 0.0))
    row = lax.broadcasted_iota(jnp.int32, (tok, tok), 0)
    column = lax.broadcasted_iota(jnp.int32, (tok, tok), 1)
    earlier = jnp.where(row < column, 1.0, 0.0).astype(BF16)
    rank = jnp.dot(has.astype(BF16), earlier, preferred_element_type=F32)
    picked = jnp.where(rank == (slot & 7).astype(F32), has, 0.0)
    tangent_slot = (slot & 8) != 0
    main = jnp.where(tangent_slot, 0.0, picked)
    slope = jnp.where(tangent_slot, picked, 0.0)
    return jnp.concatenate([main, slope], axis=1), jnp.concatenate([gate, gate], axis=1)


def kernel(
    n,
    k_hbm, dk_hbm, dq_hbm, q_hbm, v_hbm, dv_hbm, block_hbm, bits_hbm, ids_hbm, gates_hbm,
    wo_hbm, up_hbm, down_hbm,
    out_hbm, tan_hbm, dot_hbm,
    k_ref, dk_ref, dq_ref, q_ref, v_ref, dv_ref, block_ref, bits_ref, ids_ref, gates_ref,
    wo, up, down, out_ref, tan_ref, dot_ref,
    pack_send, pack_recv, probs, mix_send, mix_recv, hidden, pick, mix_high, mix_low,
    slots, rows_in, act, made, rows_back,
    load_sem, out_sem,
    pack_ss, score_rs, value_rs, mix_ss, mix_rs, disp_ss, early_rs, late_rs, back_ss, back_rs,
):
    tok = block_ref.shape[0]
    near = LENGTH // tok
    far = n - near
    owners = n // EXPERTS
    hid = up.shape[1]
    cols = D // near
    me = lax.axis_index("expert")
    pos = lax.rem(me, near)
    base = me - pos

    def send(src, dst, send_sem, recv_sem, device):
        pltpu.make_async_remote_copy(
            src_ref=src, dst_ref=dst, send_sem=send_sem, recv_sem=recv_sem,
            device_id={"expert": device}, device_id_type=MESH,
        ).start()

    def wait_bytes(ref, sem):
        pltpu.make_async_copy(ref, ref, sem).wait()

    barrier = pltpu.get_barrier_semaphore()

    def greet(device):
        pl.semaphore_signal(barrier, inc=1, device_id={"expert": device}, device_id_type=MESH)

    for k in range(1, near):
        greet(base + lax.rem(pos + k, near))

    @pl.loop(1, n // near)
    def _(g):
        greet(lax.rem(me + g * near, n))

    pairs = [
        (k_hbm, k_ref), (dk_hbm, dk_ref), (dq_hbm, dq_ref), (q_hbm, q_ref), (v_hbm, v_ref),
        (dv_hbm, dv_ref), (ids_hbm, ids_ref), (gates_hbm, gates_ref), (block_hbm, block_ref),
        (bits_hbm, bits_ref), (wo_hbm, wo), (up_hbm, up), (down_hbm, down),
    ]
    loads = [
        pltpu.make_async_copy(src, dst, load_sem.at[i]) for i, (src, dst) in enumerate(pairs)
    ]
    for load in loads:
        load.start()
    for load in loads[:6]:
        load.wait()

    parts = [ref[...] for ref in (k_ref, dk_ref, dq_ref, q_ref, v_ref, dv_ref)]
    packed = pack_send.shape[2]
    pad = jnp.zeros((tok, packed - 6 * cols), BF16)
    for j in range(near):
        pieces = []
        for pair in (parts[0:2], parts[2:4], parts[4:6]):
            for start in range(j * cols, (j + 1) * cols, HEAD_DIM):
                pieces += [part[:, start : start + HEAD_DIM] for part in pair]
        pack_send[j] = jnp.concatenate(pieces + [pad], axis=1)

    pl.semaphore_wait(barrier, near - 1 + n // near - 1)

    score_cols = -(-4 * cols // 128) * 128
    score_part = pl.ds(0, score_cols)
    value_part = pl.ds(score_cols, packed - score_cols)
    my_tokens = pl.ds(pl.multiple_of(pos * tok, tok), tok)
    for part, sem in ((score_part, score_rs), (value_part, value_rs)):

        @pl.loop(1, near)
        def _(k):
            j = lax.rem(pos + k, near)
            send(
                pack_send.at[j, :, part], pack_recv.at[my_tokens, part], pack_ss, sem, base + j
            )

    pack_recv[my_tokens, :] = pack_send[pos]

    loads[6].wait()
    loads[7].wait()
    picked, _ = slot_choice(ids_ref[...], gates_ref[...], EXPERTS * PAIR, 4)
    pick[...] = picked.astype(BF16)
    picked, gate = slot_choice(
        ids_ref[...], gates_ref[...], n * PAIR, 4 + owners.bit_length() - 1
    )
    mixing = (picked * gate).T
    high = mixing.astype(BF16)
    mix_high[...] = high
    mix_low[...] = (mixing - high.astype(F32)).astype(BF16)

    local_heads = HEADS // near
    double = 2 * HEAD_DIM
    tile = 2 * tok
    wait_bytes(pack_recv.at[pl.ds(0, (near - 1) * tok), score_part], score_rs)
    keys = [pack_recv[:, h * double : (h + 1) * double] for h in range(local_heads)]

    @pl.loop(0, near // 2, unroll=2)
    def _(i):
        rows = pl.ds(pl.multiple_of(i * tile, tile), tile)
        for h in range(local_heads):
            queries = pack_recv[rows, 2 * cols + h * double : 2 * cols + (h + 1) * double]
            alone = jnp.concatenate(
                [queries[:, HEAD_DIM:], jnp.zeros((tile, HEAD_DIM), BF16)], axis=1
            )
            both = lax.dot_general(
                keys[h], jnp.concatenate([alone, queries], axis=0),
                (((1,), (1,)), ((), ())), preferred_element_type=F32,
            )
            scores, slope = both[:, :tile], both[:, tile:]
            top = jnp.max(scores, axis=0, keepdims=True)
            exponent = jnp.exp2((scores - top) * (HEAD_DIM ** (-0.5) * LOG2E))
            inverse = 1.0 / jnp.sum(exponent, axis=0, keepdims=True)
            middle = jnp.sum(exponent * slope, axis=0, keepdims=True) * inverse
            probs[i * local_heads + h, :, :tile] = (exponent * inverse).astype(BF16)
            probs[i * local_heads + h, :, tile:] = (
                exponent * (inverse * HEAD_DIM ** (-0.5)) * (slope - middle)
            ).astype(BF16)

    wait_bytes(pack_recv.at[pl.ds(0, (near - 1) * tok), value_part], value_rs)
    tail = 4 * cols // 128 * 128
    values_t = pack_recv[:, tail:].T

    @pl.loop(0, near // 2, unroll=2)
    def _(i):
        mains, slopes = [], []
        for h in range(local_heads):
            start = 4 * cols - tail + h * double
            mixed = jnp.dot(
                values_t[start : start + double], probs[i * local_heads + h],
                preferred_element_type=F32,
            )
            mains.append(mixed[:HEAD_DIM, :tile])
            slopes.append(mixed[HEAD_DIM:, :tile] + mixed[:HEAD_DIM, tile:])
        main = jnp.concatenate(mains, axis=0)
        slope = jnp.concatenate(slopes, axis=0)
        for half in range(2):
            j = i * 2 + half
            lanes = slice(half * tok, (half + 1) * tok)
            mix_send[j] = jnp.concatenate([main[:, lanes], slope[:, lanes]], axis=1).astype(BF16)

            @pl.when(j != pos)
            def _():
                send(
                    mix_send.at[j], mix_recv.at[pl.ds(pl.multiple_of(pos * cols, 16), cols)],
                    mix_ss, mix_rs, base + j,
                )

    mix_recv[pl.ds(pl.multiple_of(pos * cols, 16), cols), :] = mix_send[pos]
    for load in loads[8:11]:
        load.wait()
    wait_bytes(mix_recv.at[pl.ds(0, (near - 1) * cols)], mix_rs)

    hidden[...] = lax.dot_general(
        mix_recv[...], wo[...], (((0,), (0,)), ((), ())), preferred_element_type=F32
    )
    signs = (2 * bits_ref[...] - 1).astype(F32)
    hidden[:tok] += block_ref[...].astype(F32)
    hidden[tok:] += signs
    normed, normed_slope = norm_pair(hidden[:tok], hidden[tok:])
    slots[...] = jnp.dot(
        pick[...],
        jnp.concatenate([normed.astype(BF16), normed_slope.astype(BF16)], axis=0),
        preferred_element_type=F32,
    ).astype(BF16)

    mine = pl.ds(pl.multiple_of(me * PAIR, PAIR), PAIR)
    half = far // 2

    def slot_rows(device):
        return pl.ds(pl.multiple_of(device // owners * PAIR, PAIR), PAIR)

    def place(u):
        return pl.ds(pl.multiple_of(u * PAIR, PAIR), PAIR)

    def partner(t, sign):
        group = lax.rem(base + n + sign * near * (1 + t // near), n)
        return group + lax.rem(pos + near + sign * lax.rem(t, near), near)

    def dispatch(t, u, sem):
        device = partner(t, 1)
        send(slots.at[slot_rows(device)], rows_in.at[place(u)], disp_ss, sem, device)

    def give_back(t, u, span):
        send(
            made.at[place(u), span], rows_back.at[mine, span],
            back_ss, back_rs, partner(t, -1),
        )

    for k in range(min(near, half)):
        dispatch(k, k, early_rs)
    for k in range(1, near):
        dispatch(far + k, half + k, early_rs)
    for k in range(half, near):
        dispatch(k, k + near, late_rs)

    @pl.loop(near, max(near, half))
    def _(t):
        dispatch(t, t, early_rs)

    @pl.loop(max(near, half), far)
    def _(t):
        dispatch(t, t + near, late_rs)

    rows_in[place(half), :] = slots[slot_rows(me), :]

    up_step = 768 if hid % 768 == 0 else hid
    every = pl.ds(0, D)

    def expert_pass(first, last, send_chunk):
        count = (last - first) * PAIR
        block = count if count <= 256 else 4 * PAIR

        @pl.loop(0, count // block)
        def _(b):
            here = pl.ds(pl.multiple_of(b * block, 16), block)
            source = pl.ds(pl.multiple_of(first * PAIR + b * block, 16), block)

            @pl.loop(0, hid // up_step, unroll=min(2, hid // up_step))
            def _(c):
                span = (
                    pl.ds(pl.multiple_of(c * up_step, 128), up_step)
                    if hid > up_step
                    else pl.ds(0, hid)
                )
                preact = jnp.dot(
                    rows_in[source, :], up[:, span], preferred_element_type=F32
                ).reshape(block // PAIR, PAIR, up_step)
                activation, derivative = gelu_pair(preact[:, :8])
                both = jnp.concatenate([activation, derivative * preact[:, 8:]], axis=1)
                act[here, span] = both.reshape(block, up_step).astype(BF16)

        for start, width in ((0, 512), (512, 512), (1024, 128)):
            span = pl.ds(start, width)

            @pl.loop(0, count // block)
            def _(b):
                here = pl.ds(pl.multiple_of(b * block, 16), block)
                target = pl.ds(pl.multiple_of(first * PAIR + b * block, 16), block)
                made[target, span] = lax.dot_general(
                    act[here, :], down[span, :], (((1,), (1,)), ((), ())),
                    preferred_element_type=F32,
                ).astype(BF16)

            send_chunk(span)

    def keep(span):
        pass

    def send_late(span):
        @pl.loop(half, far)
        def _(t):
            give_back(t, t + near, span)

    wait_bytes(rows_in.at[pl.ds(0, (half + near - 1) * PAIR)], early_rs)
    loads[11].wait()
    loads[12].wait()
    expert_pass(0, half + near, keep)
    wait_bytes(rows_in.at[pl.ds(0, (far - half) * PAIR)], late_rs)

    @pl.loop(0, half)
    def _(t):
        give_back(t, t, every)

    @pl.loop(1, near)
    def _(k):
        give_back(far + k, half + k, every)

    rows_back[mine, :] = made[place(half), :]
    expert_pass(half + near, n, send_late)
    signs = (2 * bits_ref[...] - 1).astype(F32)
    wait_bytes(rows_back.at[pl.ds(0, (n - 1) * PAIR)], back_rs)

    full = (
        hidden[...]
        + jnp.dot(mix_high[...], rows_back[...], preferred_element_type=F32)
        + jnp.dot(mix_low[...], rows_back[...], preferred_element_type=F32)
    )
    out_ref[...] = full[:tok].astype(BF16)
    full_slope = full[tok:]
    tan_ref[...] = full_slope.astype(BF16)
    column = jnp.sum(signs * full_slope, axis=1, keepdims=True) * D ** (-0.5)
    eye = lax.broadcasted_iota(jnp.int32, (tok, tok), 0) == lax.broadcasted_iota(
        jnp.int32, (tok, tok), 1
    )
    dot_ref[...] = jnp.sum(jnp.where(eye, column, 0.0), axis=0, keepdims=True)
    stores = [
        pltpu.make_async_copy(src, dst, out_sem.at[i])
        for i, (src, dst) in enumerate(
            [(out_ref, out_hbm), (tan_ref, tan_hbm), (dot_ref, dot_hbm)]
        )
    ]
    for store in stores:
        store.start()
    wait_bytes(pack_send.at[pl.ds(0, near - 1)], pack_ss)
    wait_bytes(mix_send.at[pl.ds(0, near - 1)], mix_ss)
    wait_bytes(rows_in.at[pl.ds(0, (n - 1) * PAIR)], disp_ss)
    wait_bytes(made.at[pl.ds(0, (n - 1) * PAIR)], back_ss)
    for store in stores:
        store.wait()


def place_results(a_hbm, b_hbm, c_hbm, x_hbm, y_hbm, z_hbm, a_ref, b_ref, c_ref, sem):
    moves = []
    for i, (src, held, dst) in enumerate(
        [(a_hbm, a_ref, x_hbm), (b_hbm, b_ref, y_hbm), (c_hbm, c_ref, z_hbm)]
    ):
        moves.append(
            (
                pltpu.make_async_copy(src, held, sem.at[i]),
                pltpu.make_async_copy(held, dst, sem.at[3 + i]),
            )
        )
    for load, _ in moves:
        load.start()
    for load, store in moves:
        load.wait()
        store.start()
    for _, store in moves:
        store.wait()


def per_device(
    n,
    block_input,
    probe_bits,
    query_rows,
    key_rows,
    value_rows,
    query_tangent,
    key_tangent,
    value_tangent,
    output_weight,
    expert_up,
    expert_down,
    expert_ids,
    gate_weights,
):
    tok = block_input.shape[0]
    assert tok * TOP // EXPERTS == 8
    hid = expert_up.shape[1]
    near = LENGTH // tok
    far = n - near
    cols = D // near
    packed = -(-6 * cols // 128) * 128
    anywhere = pl.BlockSpec(memory_space=pl.ANY)
    dma = pltpu.SemaphoreType.DMA
    macs = 2 * n * PAIR * D * hid + tok * D * (6 * LENGTH + 2 * D)
    results = (
        jax.ShapeDtypeStruct((tok, D), BF16),
        jax.ShapeDtypeStruct((tok, D), BF16),
        jax.ShapeDtypeStruct((1, tok), F32),
    )
    made = pl.pallas_call(
        functools.partial(kernel, n),
        out_shape=results,
        in_specs=[anywhere] * 13,
        out_specs=(anywhere,) * 3,
        scratch_shapes=[pltpu.VMEM((tok, D), BF16)] * 7
        + [
            pltpu.VMEM((tok, D), jnp.int32),
            pltpu.VMEM((TOP, tok), jnp.int32),
            pltpu.VMEM((TOP, tok), F32),
            pltpu.VMEM((D, D), BF16),
            pltpu.VMEM((D, hid), BF16),
            pltpu.VMEM((D, hid), BF16),
            pltpu.VMEM((tok, D), BF16),
            pltpu.VMEM((tok, D), BF16),
            pltpu.VMEM((1, tok), F32),
            pltpu.VMEM((near, tok, packed), BF16),
            pltpu.VMEM((LENGTH, packed), BF16),
            pltpu.VMEM((HEADS // 2, LENGTH, 4 * tok), BF16),
            pltpu.VMEM((near, cols, 2 * tok), BF16),
            pltpu.VMEM((D, 2 * tok), BF16),
            pltpu.VMEM((2 * tok, D), F32),
            pltpu.VMEM((EXPERTS * PAIR, 2 * tok), BF16),
            pltpu.VMEM((2 * tok, n * PAIR), BF16),
            pltpu.VMEM((2 * tok, n * PAIR), BF16),
            pltpu.VMEM((EXPERTS * PAIR, D), BF16),
            pltpu.VMEM((n * PAIR, D), BF16),
            pltpu.VMEM(((far // 2 + near) * PAIR, hid), BF16),
            pltpu.VMEM((n * PAIR, D), BF16),
            pltpu.VMEM((n * PAIR, D), BF16),
            dma((13,)),
            dma((3,)),
        ]
        + [dma] * 10,
        compiler_params=pltpu.CompilerParams(
            collective_id=0, has_side_effects=True, vmem_limit_bytes=56 * 1024 * 1024
        ),
        cost_estimate=pl.CostEstimate(
            flops=2 * macs, bytes_accessed=4 * D * hid + 2 * D * D, transcendentals=tok * D * 64
        ),
    )(
        key_rows, key_tangent, query_tangent, query_rows, value_rows, value_tangent,
        block_input, probe_bits, expert_ids.T, gate_weights.T,
        output_weight, expert_up, expert_down,
    )
    block_output, output_tangent, probe_dot = pl.pallas_call(
        place_results,
        out_shape=results,
        in_specs=[anywhere] * 3,
        out_specs=(anywhere,) * 3,
        scratch_shapes=[
            pltpu.VMEM((tok, D), BF16),
            pltpu.VMEM((tok, D), BF16),
            pltpu.VMEM((1, tok), F32),
            dma((6,)),
        ],
    )(*made)
    return (block_output, output_tangent, probe_dot.reshape(tok))


def solution(mesh):
    token_rows = P(("groups", "expert"), None)
    return jax.shard_map(
        functools.partial(per_device, mesh.shape["expert"]),
        mesh=mesh,
        in_specs=(token_rows,) * 8
        + (P(), P(None, "expert"), P(None, "expert"), token_rows, token_rows),
        out_specs=(token_rows, token_rows, P(("groups", "expert"))),
        check_vma=False,
    )
```
